32 devices in a mesh: gx: 4 (over y, x), gy: 2 (over core), gz: 4 (over z).
Axes of the slice: x: 2, y: 2, z: 4, core: 2. Of those that a mesh axis runs over, the one named last changes fastest.
Arguments:
- ham_blocks: bfloat16 [256, 128, 128], P(('gx', 'gy', 'gz')), may hold values from -0.119628906 to 0.119628906
- onsite: float32 [32, 768], P(('gx', 'gy', 'gz')), may hold values from -1 to 1
- entry_slot: int32 [32, 36], P(('gx', 'gy', 'gz')), may hold values from 0 to 39, as said below
- send_table: int32 [32, 8, 5], P(('gx', 'gy', 'gz')), may hold values from -1 to 7, as said below
- reads: int32 [32, 8], P(('gx', 'gy', 'gz')), may hold values from 0 to 42, as said below
- gram_targets: int32 [32, 7, 8], P(('gx', 'gy', 'gz')), may hold values from 0 to 36, as said below
- table_pick: int32 [32, 2, 8], P(('gx', 'gy', 'gz')), may hold values from 0 to 3, as said below
- phi: bfloat16 [32, 4, 128, 4096], P(('gx', 'gy', 'gz')), may hold values from -2.390625 to 2.390625
- potential_in: float32 [16, 16, 512], P('gx', 'gy', 'gz'), may hold values from -1.5 to 1.5
Outputs:
- potential: float32 [16, 16, 512], P('gx', 'gy', 'gz')
- grid_blocks: float32 [256, 128, 128], P(('gx', 'gy', 'gz'))
The draws below stay inside these ranges and needn't reach their ends.
Inputs may be any that keep to these rules, and one draw needn't show every extreme that they name: `entry_slot`: row d holds distinct slot numbers; at most 5 entries of one submatrix come from one device of its plane, and some device gives exactly 5. send_table[o, e, c] is the local block that submatrix e of o's plane reads in slot o's plane number * 5 + c, and -1 where e reads no block in that slot. `reads`: 42 marks an unused slot; some brick uses all 8 slots; the number of used slots differs widely between bricks. gram_targets[d, k, r] is 36 where slot r of the brick at face k of d is unused, and an entry below 36 where it is used; one entry of a submatrix receives at most two slots. `table_pick`: the two tables of one slot differ.
All inputs are finite; a program needn't handle non-finite values.
Results may differ from the reference program's by a relative error of at most 0.012.
Values may be sent and summed in bfloat16 or wider, within the bound.
A program may use at most 128 MiB of HBM per device.

```python
import jax
import jax.numpy as jnp
from jax import lax

B = 128
S = 6
M = 768
HB_DEV = 8
CAP = 5
RMAX = 8
NOV = 4
BX = 4
BY = 8
BZ = 128
G = 4096
NX = 16
NY = 16
NZ = 512
HBLOCKS = 256
N_GX = 4
N_GY = 2
N_GZ = 4
DEVICES = 32


SHIFTS_X = (0, -1, 1, 0, 0, 0, 0)


SHIFTS_Y = (0, 0, 0, -1, 1, 0, 0)


SHIFTS_Z = (0, 0, 0, 0, 0, -1, 1)


def neighbour_index(device, face):
    plane = N_GY * N_GZ
    coord_x = (device // plane + jnp.array(SHIFTS_X, jnp.int32)[face]) % N_GX
    coord_y = (device // N_GZ % N_GY + jnp.array(SHIFTS_Y, jnp.int32)[face]) % N_GY
    coord_z = (device % N_GZ + jnp.array(SHIFTS_Z, jnp.int32)[face]) % N_GZ
    return (coord_x * N_GY + coord_y) * N_GZ + coord_z


def request_tables(key):
    plane = N_GY * N_GZ
    count = N_GX * plane
    base = jax.random.fold_in(key, 7001)
    several = jax.random.split(base, count)
    orders = jax.vmap(lambda single: jax.random.permutation(single, plane * CAP))(several)
    positions = orders[:, :S * S].astype(jnp.int32)
    blocks = jax.random.randint(jax.random.fold_in(key, 7002), (count, S * S), 0, HB_DEV).astype(jnp.int32)
    devices = jnp.arange(count, dtype=jnp.int32)[:, None]
    owners = devices // plane * plane + positions // CAP
    targets = jnp.broadcast_to(devices % plane, positions.shape)
    lanes = positions % CAP
    table = jnp.full((count, plane, CAP), -1, jnp.int32).at[owners, targets, lanes].set(blocks)
    return (positions, table)


def reader_tables(key):
    count = DEVICES
    base = jax.random.fold_in(key, 8001)
    first = jax.random.randint(jax.random.fold_in(base, 1), (count,), 0, RMAX)
    used = 1 + first
    fullest = jax.random.randint(jax.random.fold_in(base, 3), (), 0, count)
    used = jnp.where(jnp.arange(count) == fullest, RMAX, used)
    codes = jax.random.randint(jax.random.fold_in(base, 4), (count, RMAX), 0, 7 * S).astype(jnp.int32)
    codes = jnp.where(jnp.arange(RMAX)[None, :] < used[:, None], codes, 7 * S).astype(jnp.int32)
    devices = jnp.arange(count, dtype=jnp.int32)[:, None]
    faces = jnp.arange(7, dtype=jnp.int32)[None, :]
    sources = neighbour_index(devices, faces)
    their = codes[sources]
    live = (their < 7 * S).reshape(count, 7 * RMAX).astype(jnp.int32)
    ranks = jnp.cumsum(live, axis=1) - live
    several = jax.random.split(jax.random.fold_in(base, 5), count)
    orders = jax.vmap(lambda single: jax.random.permutation(single, S * S))(several).astype(jnp.int32)
    entries = jnp.take_along_axis(orders, ranks % (S * S), axis=1)
    targets = jnp.where(live > 0, entries, S * S).astype(jnp.int32).reshape(count, 7, RMAX)
    return (codes, targets)


def draw_entry_slot(key, part):
    return request_tables(key)[0]


def draw_send_table(key, part):
    return request_tables(key)[1]


def draw_reads(key, part):
    return reader_tables(key)[0]


def draw_gram_targets(key, part):
    return reader_tables(key)[1]


def draw_table_pick(key, part):
    left = jax.random.randint(jax.random.fold_in(key, 9001), (DEVICES, RMAX), 0, NOV).astype(jnp.int32)
    step = jax.random.randint(jax.random.fold_in(key, 9002), (DEVICES, RMAX), 1, NOV).astype(jnp.int32)
    right = (left + step) % NOV
    return jnp.stack([left, right], axis=1).astype(jnp.int32)


def steps_of(stream_key, shape, shards, low, largest):
    def one(dim, parts):
        heights = jax.random.uniform(jax.random.fold_in(jax.random.fold_in(stream_key, 6), dim), (parts,), jnp.float32, low / len(shards), largest / len(shards))
        return jnp.repeat(jnp.exp(heights), shape[dim] // parts).reshape((-1,) + (1,) * (len(shape) - dim - 1))

    level = one(*shards[0])
    for cut in shards[1:]:
        level = level * one(*cut)
    return level


def noise(own_key, extent, spread, bound, cuts=(), held_as=jnp.bfloat16):
    factor_of = steps_of(own_key, extent, cuts, -0.22, 0.18) if cuts else 1.0
    values = jax.random.normal(own_key, extent, jnp.float32) * spread * factor_of
    return jnp.minimum(jnp.maximum(values, -bound), bound).astype(held_as)


def setup_inputs(seed: int = 0) -> dict:
    splits = jax.random.split(jax.random.key(seed), 10)
    ham_blocks = noise(splits[0], (HBLOCKS, B, B), 0.02, 0.119628906, ((0, 32),))
    onsite = jnp.clip(jax.random.uniform(splits[1], (DEVICES, M), jnp.float32, -1.0, 1.0) * steps_of(splits[1], (DEVICES, M), ((0, 32),), -0.4, 0.0), -1.0, 1.0)
    entry_slot = draw_entry_slot(jax.random.fold_in(splits[9], 71), 0)
    send_table = draw_send_table(jax.random.fold_in(splits[9], 71), 0)
    reads = draw_reads(jax.random.fold_in(splits[9], 71), 0)
    gram_targets = draw_gram_targets(jax.random.fold_in(splits[9], 71), 0)
    table_pick = draw_table_pick(jax.random.fold_in(splits[9], 71), 0)
    phi = noise(splits[7], (DEVICES, NOV, B, G), 0.4, 2.390625, ((0, 32),))
    potential_in = noise(splits[8], (NX, NY, NZ), 0.25, 1.5, ((0, 4), (1, 2), (2, 4)), jnp.float32)
    return dict(ham_blocks=ham_blocks, onsite=onsite, entry_slot=entry_slot, send_table=send_table, reads=reads, gram_targets=gram_targets, table_pick=table_pick, phi=phi, potential_in=potential_in)


SHIFTS_X = (0, -1, 1, 0, 0, 0, 0)
SHIFTS_Y = (0, 0, 0, -1, 1, 0, 0)
SHIFTS_Z = (0, 0, 0, 0, 0, -1, 1)
EPSILON = 1e-06

def neighbour(device, face):
    plane = N_GY * N_GZ
    coord_x = device // plane
    coord_y = device // N_GZ % N_GY
    coord_z = device % N_GZ
    coord_x = (coord_x + jnp.array(SHIFTS_X, jnp.int32)[face]) % N_GX
    coord_y = (coord_y + jnp.array(SHIFTS_Y, jnp.int32)[face]) % N_GY
    coord_z = (coord_z + jnp.array(SHIFTS_Z, jnp.int32)[face]) % N_GZ
    return (coord_x * N_GY + coord_y) * N_GZ + coord_z

def assemble(device, ham_blocks, entry_slot, send_table):
    plane = N_GY * N_GZ
    positions = entry_slot[device]
    owners = device // plane * plane + positions // CAP
    chosen = send_table[owners, device % plane, positions % CAP]
    blocks = ham_blocks[owners * HB_DEV + chosen]
    return blocks.reshape(S, S, B, B).transpose(0, 2, 1, 3).reshape(M, M)

def density_columns(matrix, onsite_row):
    wide = matrix.astype(jnp.float32)
    hamilton = 0.5 * (wide + wide.T) + jnp.diag(onsite_row.astype(jnp.float32))
    factor = lax.rsqrt(jnp.sum(hamilton * hamilton) / M + EPSILON) / 1.3
    start = (hamilton * factor).astype(jnp.bfloat16)
    square = jnp.dot(start, start, preferred_element_type=jnp.float32).astype(jnp.bfloat16)
    cube = jnp.dot(start, square, preferred_element_type=jnp.float32)
    first = (1.5 * start.astype(jnp.float32) - 0.5 * cube).astype(jnp.bfloat16)
    column = first[:, :B]
    inner = jnp.dot(first, column, preferred_element_type=jnp.float32).astype(jnp.bfloat16)
    outer = jnp.dot(first, inner, preferred_element_type=jnp.float32)
    unit = (jnp.arange(M)[:, None] == jnp.arange(B)[None, :]).astype(jnp.float32)
    result = 0.5 * (unit - (1.5 * column.astype(jnp.float32) - 0.5 * outer))
    return result.astype(jnp.bfloat16).reshape(S, B, B)

def jacobi(field, source):
    beside_all = jnp.roll(field, -1, 0) + jnp.roll(field, 1, 0)
    beside_all = beside_all + jnp.roll(field, -1, 1) + jnp.roll(field, 1, 1)
    beside_all = beside_all + jnp.roll(field, -1, 2) + jnp.roll(field, 1, 2)
    return (beside_all + source) / 6.0

def reference(ham_blocks, onsite, entry_slot, send_table, reads, gram_targets, table_pick, phi, potential_in):
    plane = N_GY * N_GZ
    devices = jnp.arange(DEVICES, dtype=jnp.int32)

    def one_submatrix(device):
        return density_columns(assemble(device, ham_blocks, entry_slot, send_table), onsite[device])
    density = lax.map(one_submatrix, devices)
    candidates = jnp.concatenate([density.reshape(DEVICES * S, B, B), jnp.zeros((1, B, B), density.dtype)])

    def one_brick(device):
        codes = reads[device]
        live = codes < 7 * S
        faces = jnp.where(live, codes // S, 0)
        sources = neighbour(device, faces)
        index = jnp.where(live, sources * S + codes % S, DEVICES * S)
        blocks = candidates[index].astype(jnp.float32)
        left_table = phi[device][table_pick[device, 0]].astype(jnp.float32)
        right_table = phi[device][table_pick[device, 1]].astype(jnp.float32)
        mixed = jnp.einsum('rij,rig->rjg', blocks, left_table, precision=lax.Precision.HIGHEST)
        return lax.optimization_barrier(jnp.sum(mixed * right_table, axis=(0, 1)))
    brick_rho = lax.map(one_brick, devices)
    source = brick_rho.reshape(N_GX, N_GY, N_GZ, BX, BY, BZ).transpose(0, 3, 1, 4, 2, 5).reshape(NX, NY, NZ)
    potential = potential_in
    for sweep_index in range(2):
        potential = jacobi(potential, source)
    bricks = potential.reshape(N_GX, BX, N_GY, BY, N_GZ, BZ).transpose(0, 2, 4, 1, 3, 5).reshape(DEVICES, G)

    def one_gram(device):
        left_table = phi[device][table_pick[device, 0]].astype(jnp.float32)
        scaled = (phi[device][table_pick[device, 1]].astype(jnp.float32) * bricks[device][None, None, :]).astype(jnp.bfloat16)
        scaled = lax.optimization_barrier(scaled).astype(jnp.float32)
        return jnp.einsum('rig,rjg->rij', left_table, scaled, precision=lax.Precision.HIGHEST).astype(jnp.bfloat16)
    gram_all = lax.map(one_gram, devices)

    def one_return(device):
        sources = neighbour(device, jnp.arange(7, dtype=jnp.int32))
        pieces = gram_all[sources].reshape(7 * RMAX, B, B).astype(jnp.float32)
        selector = (gram_targets[device].reshape(-1)[None, :] == jnp.arange(S * S, dtype=jnp.int32)[:, None]).astype(jnp.float32)
        return jnp.einsum('sq,qij->sij', selector, pieces, precision=lax.Precision.HIGHEST).astype(jnp.bfloat16)
    positions = entry_slot
    owners = devices[:, None] // plane * plane + positions // CAP
    chosen = send_table[owners, (devices % plane)[:, None], positions % CAP]
    target = (owners * HB_DEV + chosen).astype(jnp.int32)

    def add_returned(device, total):
        piece = one_return(device).astype(jnp.float32)
        return total.at[target[device]].add(piece)
    grid_blocks = lax.fori_loop(0, DEVICES, add_returned, jnp.zeros((HBLOCKS, B, B), jnp.float32))
    return (potential, grid_blocks)
```

```python
import functools

import jax
import jax.numpy as jnp
from jax import lax
from jax.experimental import pallas as pl
from jax.experimental.pallas import tpu as pltpu
from jax.sharding import PartitionSpec as P

EPSILON = 1e-06
PLANE = ("gy", "gz")
EVERY = ("gx", "gy", "gz")
VMEM_LIMIT = 48 * 1024 * 1024
VMEM = pl.BlockSpec(memory_space=pltpu.VMEM)
SMEM = pl.BlockSpec(memory_space=pltpu.SMEM)


def local_call(kernel, out_shape, in_specs, scratch=(), flops=0, moved=0):
    return pl.pallas_call(
        kernel,
        out_shape=out_shape,
        in_specs=in_specs,
        out_specs=VMEM,
        scratch_shapes=scratch,
        compiler_params=pltpu.CompilerParams(vmem_limit_bytes=VMEM_LIMIT),
        cost_estimate=pl.CostEstimate(flops=flops, bytes_accessed=moved, transcendentals=0),
    )


def density_kernel(side, bins_ref, blocks_ref, onsite_ref, out_ref, h_ref, x_ref, q_ref):
    width = blocks_ref.shape[1]
    order = side * width
    rows = lax.broadcasted_iota(jnp.int32, (width, width), 0)
    columns = lax.broadcasted_iota(jnp.int32, (width, width), 1)
    unit = rows == columns
    total = jnp.zeros((width, width), jnp.float32)
    for s in range(side):
        for t in range(s, side):
            upper = blocks_ref[bins_ref[s * side + t]].astype(jnp.float32)
            lower = blocks_ref[bins_ref[t * side + s]].astype(jnp.float32)
            block = 0.5 * (upper + lower.T)
            here, there = pl.ds(s * width, width), pl.ds(t * width, width)
            if s == t:
                block = block + jnp.where(unit, onsite_ref[:, here], 0.0)
                total = total + block * block
            else:
                total = total + 2.0 * (block * block)
                h_ref[there, here] = block.T
            h_ref[here, there] = block
    norm = jnp.sum(jnp.sum(total, axis=0, keepdims=True), axis=1, keepdims=True)
    factor = lax.rsqrt(norm / order + EPSILON) / 1.3
    for s in range(side):
        here = pl.ds(s * width, width)
        x_ref[here, :] = (h_ref[here, :] * factor).astype(jnp.bfloat16)
    step = 256 if order % 256 == 0 else width
    for c in range(order // step):
        here = pl.ds(c * step, step)
        q_ref[:, here] = jnp.dot(
            x_ref[...], x_ref[:, here], preferred_element_type=jnp.float32
        ).astype(jnp.bfloat16)
    for c in range(order // step):
        here = pl.ds(c * step, step)
        h_ref[:, here] = 1.5 * x_ref[:, here].astype(jnp.float32) - 0.5 * jnp.dot(
            x_ref[...], q_ref[:, here], preferred_element_type=jnp.float32
        )
    for c in range(order // step):
        here = pl.ds(c * step, step)
        q_ref[:, here] = h_ref[:, here].astype(jnp.bfloat16)
    first = q_ref[...]
    column = q_ref[:, :width]
    inner = jnp.dot(first, column, preferred_element_type=jnp.float32).astype(jnp.bfloat16)
    outer = jnp.dot(first, inner, preferred_element_type=jnp.float32)
    result = -0.5 * (1.5 * column.astype(jnp.float32) - 0.5 * outer)
    for s in range(side):
        part = result[s * width : (s + 1) * width, :]
        if s == 0:
            part = part + jnp.where(unit, 0.5, 0.0)
        out_ref[s] = part.astype(jnp.bfloat16)


def source_kernel(reads_ref, pick_ref, blocks_ref, phi_ref, out_ref, p_ref, pb_ref):
    width = blocks_ref.shape[1]
    count = blocks_ref.shape[0]
    tables = phi_ref.shape[0]
    points = phi_ref.shape[2]
    p_ref[...] = jnp.zeros_like(p_ref)
    for r in range(reads_ref.shape[0]):
        code = reads_ref[r]

        @pl.when(code < count)
        def _():
            place = pick_ref[0, r] * tables + pick_ref[1, r]
            p_ref[place] = p_ref[place] + blocks_ref[code].astype(jnp.float32)

    for a in range(tables):
        for b in range(tables):
            pb_ref[a * width : (a + 1) * width, b * width : (b + 1) * width] = p_ref[
                a * tables + b
            ].astype(jnp.bfloat16)
    step = 512

    def body(c, carry):
        here = pl.ds(pl.multiple_of(c * step, step), step)
        cells = phi_ref[:, :, here].reshape(tables * width, step)
        mixed = jnp.dot(pb_ref[...], cells, preferred_element_type=jnp.float32)
        line = jnp.sum(mixed * cells.astype(jnp.float32), axis=0, keepdims=True)
        for j in range(step // 128):
            out_ref[pl.ds(c * (step // 128) + j, 1), :] = line[:, j * 128 : (j + 1) * 128]
        return carry

    lax.fori_loop(0, points // step, body, 0)


def pairs_of(tables):
    return [(a, b) for a in range(tables) for b in range(a + 1, tables)]


def gram_kernel(phi_ref, v_ref, out_ref, g_ref):
    tables, width, points = phi_ref.shape
    step = 512
    g_ref[...] = jnp.zeros_like(g_ref)
    size = (tables - 1) * width

    def body(c, carry):
        here = pl.ds(pl.multiple_of(c * step, step), step)
        rows = v_ref[pl.ds(c * (step // 128), step // 128), :]
        line = jnp.concatenate([rows[j : j + 1, :] for j in range(step // 128)], axis=1)
        right = phi_ref[1:, :, here].reshape(size, step).astype(jnp.float32)
        weighted = (right * line).astype(jnp.bfloat16)
        left = phi_ref[: tables - 1, :, here].reshape(size, step)
        g_ref[...] += lax.dot_general(
            left, weighted, (((1,), (1,)), ((), ())), preferred_element_type=jnp.float32
        )
        return carry

    lax.fori_loop(0, points // step, body, 0)
    for n, (a, b) in enumerate(pairs_of(tables)):
        out_ref[n] = g_ref[
            a * width : (a + 1) * width, (b - 1) * width : b * width
        ].astype(jnp.bfloat16)


def combine_kernel(bin_ref, col_ref, flip_ref, blocks_ref, out_ref, acc_ref):
    bins = out_ref.shape[0]
    acc_ref[...] = jnp.zeros_like(acc_ref)

    def body(n, carry):
        place = bin_ref[n]

        @pl.when((place < bins) & (flip_ref[n] == 0))
        def _():
            acc_ref[place] = acc_ref[place] + blocks_ref[col_ref[n]].astype(jnp.float32)

        @pl.when((place < bins) & (flip_ref[n] == 1))
        def _():
            acc_ref[place] = acc_ref[place] + blocks_ref[col_ref[n]].astype(jnp.float32).T

        return carry

    lax.fori_loop(0, bin_ref.shape[0], body, 0)
    out_ref[...] = acc_ref[...].astype(jnp.bfloat16)


def both_sides(low_part, high_part, axis):
    count = lax.axis_size(axis)
    if count == 1:
        return high_part, low_part
    up = [(i, (i + 1) % count) for i in range(count)]
    down = [((i + 1) % count, i) for i in range(count)]
    below = lax.ppermute(high_part, axis, up)
    if count == 2 and low_part is high_part:
        return below, below
    return below, lax.ppermute(low_part, axis, down)


def face_stack(block):
    parts = [block]
    for axis in EVERY:
        parts.extend(both_sides(block, block, axis))
    return jnp.concatenate(parts)


def faces_of(field):
    got = []
    for dim, axis in enumerate(EVERY):
        size = field.shape[dim]
        low = lax.slice_in_dim(field, 0, 1, axis=dim)
        high = lax.slice_in_dim(field, size - 1, size, axis=dim)
        got.append(both_sides(low, high, axis))
    return got


def jacobi_step(field, faces, source):
    beside_all = source
    for dim in range(3):
        below, above = faces[dim]
        size = field.shape[dim]
        beside_all = beside_all + jnp.concatenate(
            [below, lax.slice_in_dim(field, 0, size - 1, axis=dim)], axis=dim
        )
        beside_all = beside_all + jnp.concatenate(
            [lax.slice_in_dim(field, 1, size, axis=dim), above], axis=dim
        )
    return beside_all / 6.0


def neighbour_numbers():
    counts = [lax.axis_size(axis) for axis in EVERY]
    here = [lax.axis_index(axis) for axis in EVERY]
    places = []
    for shift in (
        (0, 0, 0), (-1, 0, 0), (1, 0, 0), (0, -1, 0), (0, 1, 0), (0, 0, -1), (0, 0, 1)
    ):
        x, y, z = [(h + s + n) % n for h, s, n in zip(here, shift, counts)]
        places.append((x * counts[1] + y) * counts[2] + z)
    return jnp.stack(places)


def gather_plane(blocks):
    return lax.all_gather(blocks, PLANE, axis=0, tiled=True)


def scatter_plane(partial):
    return lax.psum_scatter(partial, PLANE, scatter_dimension=0, tiled=True)


def shards(
    ham_blocks, onsite, entry_slot, send_table, reads, gram_targets, table_pick, phi, potential_in
):
    plane = lax.axis_size(PLANE)
    held, width, _ = ham_blocks.shape
    lanes_count = send_table.shape[2]
    order = onsite.shape[1]
    side = order // width
    tables = phi.shape[1]
    points = phi.shape[3]
    slots = reads.shape[1]
    pairs = pairs_of(tables)

    gathered = gather_plane(ham_blocks)
    sent_numbers = plane * lanes_count
    numbers = jnp.concatenate([send_table.reshape(1, -1), table_pick.reshape(1, -1)], axis=1)
    numbers = lax.all_gather(numbers, EVERY, axis=0, tiled=True)
    mine = lax.axis_index(PLANE)
    owners = lax.axis_index("gx") * plane + jnp.arange(plane)
    theirs = jnp.take(numbers, owners, axis=0)[:, :sent_numbers]
    theirs = jnp.take(theirs.reshape(plane, plane, lanes_count), mine, axis=1)
    chosen = jnp.take(theirs.reshape(-1), entry_slot[0])
    bins = ((entry_slot[0] // lanes_count) * held + chosen).astype(jnp.int32)

    density = local_call(
        functools.partial(density_kernel, side),
        jax.ShapeDtypeStruct((side, width, width), jnp.bfloat16),
        [SMEM, VMEM, VMEM],
        [
            pltpu.VMEM((order, order), jnp.float32),
            pltpu.VMEM((order, order), jnp.bfloat16),
            pltpu.VMEM((order, order), jnp.bfloat16),
        ],
        flops=4 * order**3,
        moved=gathered.size * 2,
    )(bins, gathered, onsite)
    candidates = face_stack(density)
    first_faces = faces_of(potential_in)
    source = local_call(
        source_kernel,
        jax.ShapeDtypeStruct((points // 128, 128), jnp.float32),
        [SMEM, SMEM, VMEM, VMEM],
        [
            pltpu.VMEM((tables * tables, width, width), jnp.float32),
            pltpu.VMEM((tables * width, tables * width), jnp.bfloat16),
        ],
        flops=2 * points * (tables * width) ** 2,
        moved=phi.size * 2,
    )(reads[0], table_pick[0], candidates, phi[0]).reshape(potential_in.shape)
    potential = jacobi_step(potential_in, first_faces, source)
    potential = jacobi_step(potential, faces_of(potential), source)
    grams = local_call(
        gram_kernel,
        jax.ShapeDtypeStruct((len(pairs), width, width), jnp.bfloat16),
        [VMEM, VMEM],
        [pltpu.VMEM(((tables - 1) * width, (tables - 1) * width), jnp.float32)],
        flops=2 * points * (tables * width) ** 2,
        moved=phi.size * 2,
    )(phi[0], potential.reshape(points // 128, 128))
    gathered_grams = face_stack(grams)

    near = jnp.take(numbers, neighbour_numbers(), axis=0)[:, sent_numbers:]
    near = near.reshape(7, 2, slots)
    low = jnp.minimum(near[:, 0], near[:, 1])
    high = jnp.maximum(near[:, 0], near[:, 1])
    pair = low * tables - low * (low + 1) // 2 + high - low - 1
    column = (jnp.arange(7)[:, None] * len(pairs) + pair).reshape(-1).astype(jnp.int32)
    flip = (near[:, 0] > near[:, 1]).reshape(-1).astype(jnp.int32)
    padded = jnp.concatenate([bins, jnp.full((1,), plane * held, jnp.int32)])
    place = jnp.take(padded, gram_targets[0].reshape(-1))
    partial = local_call(
        combine_kernel,
        jax.ShapeDtypeStruct((plane * held, width, width), jnp.bfloat16),
        [SMEM, SMEM, SMEM, VMEM],
        [pltpu.VMEM((plane * held, width, width), jnp.float32)],
        flops=7 * slots * width * width,
        moved=plane * held * width * width * 2,
    )(place, column, flip, gathered_grams)
    grid_blocks = scatter_plane(partial).astype(jnp.float32)
    return (potential, grid_blocks)


def solution(mesh):
    placed = (
        P(EVERY, None, None),
        P(EVERY, None),
        P(EVERY, None),
        P(EVERY, None, None),
        P(EVERY, None),
        P(EVERY, None, None),
        P(EVERY, None, None),
        P(EVERY, None, None, None),
        P(*EVERY),
    )
    return jax.shard_map(
        shards,
        mesh=mesh,
        in_specs=placed,
        out_specs=(P(*EVERY), P(EVERY, None, None)),
        check_vma=False,
    )
```

```python
import functools

import jax
import jax.numpy as jnp
from jax import lax
from jax.experimental import pallas as pl
from jax.experimental.pallas import tpu as pltpu
from jax.sharding import PartitionSpec as P

EPSILON = 1e-06
PLANE = ("gy", "gz")
EVERY = ("gx", "gy", "gz")
VMEM_LIMIT = 48 * 1024 * 1024
VMEM = pl.BlockSpec(memory_space=pltpu.VMEM)
SMEM = pl.BlockSpec(memory_space=pltpu.SMEM)
MESH = pl.DeviceIdType.MESH


def local_call(kernel, out_shape, in_specs, scratch=(), flops=0, moved=0):
    return pl.pallas_call(
        kernel,
        out_shape=out_shape,
        in_specs=in_specs,
        out_specs=VMEM,
        scratch_shapes=scratch,
        compiler_params=pltpu.CompilerParams(vmem_limit_bytes=VMEM_LIMIT),
        cost_estimate=pl.CostEstimate(flops=flops, bytes_accessed=moved, transcendentals=0),
    )


def density_kernel(side, bins_ref, blocks_ref, onsite_ref, out_ref, h_ref, x_ref, q_ref):
    width = blocks_ref.shape[1]
    order = side * width
    rows = lax.broadcasted_iota(jnp.int32, (width, width), 0)
    columns = lax.broadcasted_iota(jnp.int32, (width, width), 1)
    unit = rows == columns
    total = jnp.zeros((width, width), jnp.float32)
    for s in range(side):
        for t in range(s, side):
            upper = blocks_ref[bins_ref[s * side + t]].astype(jnp.float32)
            lower = blocks_ref[bins_ref[t * side + s]].astype(jnp.float32)
            block = 0.5 * (upper + lower.T)
            here, there = pl.ds(s * width, width), pl.ds(t * width, width)
            if s == t:
                block = block + jnp.where(unit, onsite_ref[:, here], 0.0)
                total = total + block * block
            else:
                total = total + 2.0 * (block * block)
                h_ref[there, here] = block.T
            h_ref[here, there] = block
    norm = jnp.sum(jnp.sum(total, axis=0, keepdims=True), axis=1, keepdims=True)
    factor = lax.rsqrt(norm / order + EPSILON) / 1.3
    for s in range(side):
        here = pl.ds(s * width, width)
        x_ref[here, :] = (h_ref[here, :] * factor).astype(jnp.bfloat16)
    step = 256 if order % 256 == 0 else width
    for c in range(order // step):
        here = pl.ds(c * step, step)
        q_ref[:, here] = jnp.dot(
            x_ref[...], x_ref[:, here], preferred_element_type=jnp.float32
        ).astype(jnp.bfloat16)
    for c in range(order // step):
        here = pl.ds(c * step, step)
        h_ref[:, here] = 1.5 * x_ref[:, here].astype(jnp.float32) - 0.5 * jnp.dot(
            x_ref[...], q_ref[:, here], preferred_element_type=jnp.float32
        )
    for c in range(order // step):
        here = pl.ds(c * step, step)
        q_ref[:, here] = h_ref[:, here].astype(jnp.bfloat16)
    first = q_ref[...]
    column = q_ref[:, :width]
    inner = jnp.dot(first, column, preferred_element_type=jnp.float32).astype(jnp.bfloat16)
    outer = jnp.dot(first, inner, preferred_element_type=jnp.float32)
    result = -0.5 * (1.5 * column.astype(jnp.float32) - 0.5 * outer)
    for s in range(side):
        part = result[s * width : (s + 1) * width, :]
        if s == 0:
            part = part + jnp.where(unit, 0.5, 0.0)
        out_ref[s] = part.astype(jnp.bfloat16)


def source_kernel(reads_ref, pick_ref, blocks_ref, phi_ref, out_ref, p_ref, pb_ref):
    width = blocks_ref.shape[1]
    count = blocks_ref.shape[0]
    tables = phi_ref.shape[0]
    points = phi_ref.shape[2]
    p_ref[...] = jnp.zeros_like(p_ref)
    for r in range(reads_ref.shape[0]):
        code = reads_ref[r]

        @pl.when(code < count)
        def _():
            place = pick_ref[0, r] * tables + pick_ref[1, r]
            p_ref[place] = p_ref[place] + blocks_ref[code].astype(jnp.float32)

    for a in range(tables):
        for b in range(tables):
            pb_ref[a * width : (a + 1) * width, b * width : (b + 1) * width] = p_ref[
                a * tables + b
            ].astype(jnp.bfloat16)
    step = 512

    def body(c, carry):
        here = pl.ds(pl.multiple_of(c * step, step), step)
        cells = phi_ref[:, :, here].reshape(tables * width, step)
        mixed = jnp.dot(pb_ref[...], cells, preferred_element_type=jnp.float32)
        line = jnp.sum(mixed * cells.astype(jnp.float32), axis=0, keepdims=True)
        for j in range(step // 128):
            out_ref[pl.ds(c * (step // 128) + j, 1), :] = line[:, j * 128 : (j + 1) * 128]
        return carry

    lax.fori_loop(0, points // step, body, 0)


def pairs_of(tables):
    return [(a, b) for a in range(tables) for b in range(a + 1, tables)]


def gram_kernel(phi_ref, v_ref, out_ref, g_ref):
    tables, width, points = phi_ref.shape
    step = 512
    g_ref[...] = jnp.zeros_like(g_ref)
    size = (tables - 1) * width

    def body(c, carry):
        here = pl.ds(pl.multiple_of(c * step, step), step)
        rows = v_ref[pl.ds(c * (step // 128), step // 128), :]
        line = jnp.concatenate([rows[j : j + 1, :] for j in range(step // 128)], axis=1)
        right = phi_ref[1:, :, here].reshape(size, step).astype(jnp.float32)
        weighted = (right * line).astype(jnp.bfloat16)
        left = phi_ref[: tables - 1, :, here].reshape(size, step)
        g_ref[...] += lax.dot_general(
            left, weighted, (((1,), (1,)), ((), ())), preferred_element_type=jnp.float32
        )
        return carry

    lax.fori_loop(0, points // step, body, 0)
    for n, (a, b) in enumerate(pairs_of(tables)):
        out_ref[n] = g_ref[
            a * width : (a + 1) * width, (b - 1) * width : b * width
        ].astype(jnp.bfloat16)


def combine_kernel(bin_ref, col_ref, flip_ref, blocks_ref, out_ref, acc_ref):
    bins = out_ref.shape[0]
    acc_ref[...] = jnp.zeros_like(acc_ref)

    def body(n, carry):
        place = bin_ref[n]

        @pl.when((place < bins) & (flip_ref[n] == 0))
        def _():
            acc_ref[place] = acc_ref[place] + blocks_ref[col_ref[n]].astype(jnp.float32)

        @pl.when((place < bins) & (flip_ref[n] == 1))
        def _():
            acc_ref[place] = acc_ref[place] + blocks_ref[col_ref[n]].astype(jnp.float32).T

        return carry

    lax.fori_loop(0, bin_ref.shape[0], body, 0)
    out_ref[...] = acc_ref[...].astype(jnp.bfloat16)


def both_sides(low_part, high_part, axis):
    count = lax.axis_size(axis)
    if count == 1:
        return high_part, low_part
    up = [(i, (i + 1) % count) for i in range(count)]
    down = [((i + 1) % count, i) for i in range(count)]
    below = lax.ppermute(high_part, axis, up)
    if count == 2 and low_part is high_part:
        return below, below
    return below, lax.ppermute(low_part, axis, down)


def face_stack(block):
    parts = [block]
    for axis in EVERY:
        parts.extend(both_sides(block, block, axis))
    return jnp.concatenate(parts)


def faces_of(field):
    got = []
    for dim, axis in enumerate(EVERY):
        size = field.shape[dim]
        low = lax.slice_in_dim(field, 0, 1, axis=dim)
        high = lax.slice_in_dim(field, size - 1, size, axis=dim)
        got.append(both_sides(low, high, axis))
    return got


def jacobi_step(field, faces, source):
    beside_all = source
    for dim in range(3):
        below, above = faces[dim]
        size = field.shape[dim]
        beside_all = beside_all + jnp.concatenate(
            [below, lax.slice_in_dim(field, 0, size - 1, axis=dim)], axis=dim
        )
        beside_all = beside_all + jnp.concatenate(
            [lax.slice_in_dim(field, 1, size, axis=dim), above], axis=dim
        )
    return beside_all / 6.0


def neighbour_numbers():
    rows, line = lax.axis_size("gy"), lax.axis_size("gz")
    row, z = lax.axis_index("gy"), lax.axis_index("gz")
    places = []
    for i, k in ((-1, 0), (1, 0), (0, -1), (0, 1)):
        places.append((row + i + rows) % rows * line + (z + k + line) % line)
    return jnp.stack(places)


def greet_plane(line, group, z, row):
    barrier = pltpu.get_barrier_semaphore()

    @pl.when(z > 0)
    def _():
        pl.semaphore_signal(barrier, inc=1, device_id={"gz": z - 1}, device_id_type=MESH)

    @pl.when(z < line - 1)
    def _():
        pl.semaphore_signal(barrier, inc=1, device_id={"gz": z + 1}, device_id_type=MESH)

    for j in range(1, group):
        pl.semaphore_signal(
            barrier, inc=1, device_id={"gy": lax.rem(row + j, group)}, device_id_type=MESH
        )

    below = lax.div(z + line - 1, line)
    above = lax.div(2 * line - 2 - z, line)
    pl.semaphore_wait(barrier, group - 1 + below + above)


def pieces_of(count):
    return 4 if count % 4 == 0 else 1


def gather_kernel(
    line, group, x_ref, n_ref, out_ref, nout_ref, line_send, line_recv, row_send, row_recv
):
    z, row = lax.axis_index("gz"), lax.axis_index("gy")
    held, tall = x_ref.shape[0], n_ref.shape[0]
    pieces = pieces_of(held)
    part = held // pieces

    def slot(owner_row, owner_z, c):
        owner = owner_row * line + owner_z
        if c < pieces:
            return out_ref.at[pl.ds(owner * held + c * part, part)]
        return nout_ref.at[pl.ds(pl.multiple_of(owner * tall, tall), tall)]

    def source(c):
        return x_ref.at[pl.ds(c * part, part)] if c < pieces else n_ref

    def along(origin, c, side, own):
        return pltpu.make_async_remote_copy(
            src_ref=source(c) if own else slot(row, origin, c),
            dst_ref=slot(row, origin, c),
            send_sem=line_send.at[side, origin, c],
            recv_sem=line_recv.at[origin, c],
            device_id={"gz": z + 1 if side == 0 else z - 1},
            device_id_type=MESH,
        )

    def across(j, origin, kind, own):
        owner = row * line + origin
        if kind == 0:
            dst = out_ref.at[pl.ds(owner * held, held)]
            src = x_ref if own else dst
        else:
            dst = nout_ref.at[pl.ds(pl.multiple_of(owner * tall, tall), tall)]
            src = n_ref if own else dst
        return pltpu.make_async_remote_copy(
            src_ref=src,
            dst_ref=dst,
            send_sem=row_send.at[j - 1, origin, kind],
            recv_sem=row_recv.at[j - 1, origin, kind],
            device_id={"gy": lax.rem(row + j, group)},
            device_id_type=MESH,
        )

    def arrived(j, origin, kind):
        owner = lax.rem(row + group - j, group) * line + origin
        if kind == 0:
            dst = out_ref.at[pl.ds(owner * held, held)]
        else:
            dst = nout_ref.at[pl.ds(pl.multiple_of(owner * tall, tall), tall)]
        return pltpu.make_async_remote_copy(
            src_ref=dst,
            dst_ref=dst,
            send_sem=row_send.at[j - 1, origin, kind],
            recv_sem=row_recv.at[j - 1, origin, kind],
            device_id={"gy": lax.rem(row + j, group)},
            device_id_type=MESH,
        )

    greet_plane(line, group, z, row)
    order = [pieces] + list(range(pieces))
    for c in order:

        @pl.when(z < line - 1)
        def _():
            along(z, c, 0, True).start()

        @pl.when(z > 0)
        def _():
            along(z, c, 1, True).start()

    for j in range(1, group):
        for kind in range(2):
            across(j, z, kind, True).start()
    mine = row * line + z
    out_ref[pl.ds(mine * held, held)] = x_ref[...]
    nout_ref[pl.ds(pl.multiple_of(mine * tall, tall), tall), :] = n_ref[...]
    for s in range(1, line):
        for c in order:

            @pl.when(z >= s)
            def _():
                along(z - s, c, 0, False).wait_recv()

            @pl.when((z >= s) & (z < line - 1))
            def _():
                along(z - s, c, 0, False).start()

            @pl.when(z + s < line)
            def _():
                along(z + s, c, 1, False).wait_recv()

            @pl.when((z + s < line) & (z > 0))
            def _():
                along(z + s, c, 1, False).start()

        for j in range(1, group):
            for kind in range(2):

                @pl.when(z >= s)
                def _():
                    across(j, z - s, kind, False).start()

                @pl.when(z + s < line)
                def _():
                    across(j, z + s, kind, False).start()

    for j in range(1, group):
        for origin in range(line):
            for kind in range(2):
                arrived(j, origin, kind).wait_recv()
                across(j, origin, kind, False).wait_send()
    for s in range(line):
        for c in order:

            @pl.when((z >= s) & (z < line - 1))
            def _():
                along(z - s, c, 0, False).wait_send()

            @pl.when((z + s < line) & (z > 0))
            def _():
                along(z + s, c, 1, False).wait_send()


def gather_plane(blocks, numbers):
    line, group = lax.axis_size("gz"), lax.axis_size("gy")
    plane = line * group
    kinds = pieces_of(blocks.shape[0]) + 1
    others = max(group - 1, 1)
    return pl.pallas_call(
        functools.partial(gather_kernel, line, group),
        out_shape=(
            jax.ShapeDtypeStruct((plane * blocks.shape[0],) + blocks.shape[1:], blocks.dtype),
            jax.ShapeDtypeStruct((plane * numbers.shape[0], numbers.shape[1]), numbers.dtype),
        ),
        in_specs=[VMEM, VMEM],
        out_specs=(VMEM, VMEM),
        scratch_shapes=[
            pltpu.SemaphoreType.DMA((2, line, kinds)),
            pltpu.SemaphoreType.DMA((line, kinds)),
            pltpu.SemaphoreType.DMA((others, line, 2)),
            pltpu.SemaphoreType.DMA((others, line, 2)),
        ],
        compiler_params=pltpu.CompilerParams(
            collective_id=1, has_side_effects=True, vmem_limit_bytes=VMEM_LIMIT
        ),
    )(blocks, numbers)


def scatter_kernel(
    line, group, x_ref, out_ref, row_buf, acc_buf, pass_buf,
    row_send, row_recv, line_send, line_recv,
):
    z, row = lax.axis_index("gz"), lax.axis_index("gy")
    held = out_ref.shape[0]
    pieces = pieces_of(held)
    part = held // pieces
    f32 = jnp.float32

    def across(j, target):
        peer = lax.rem(row + j, group)
        return pltpu.make_async_remote_copy(
            src_ref=x_ref.at[pl.ds((peer * line + target) * held, held)],
            dst_ref=row_buf.at[j - 1, target],
            send_sem=row_send.at[j - 1, target],
            recv_sem=row_recv.at[j - 1, target],
            device_id={"gy": peer},
            device_id_type=MESH,
        )

    def along(side, target, c):
        piece = pass_buf.at[side, target, pl.ds(c * part, part)]
        return pltpu.make_async_remote_copy(
            src_ref=piece,
            dst_ref=piece,
            send_sem=line_send.at[side, target, c],
            recv_sem=line_recv.at[side, target, c],
            device_id={"gz": z + 1 if side == 0 else z - 1},
            device_id_type=MESH,
        )

    greet_plane(line, group, z, row)
    turn = []
    for k in range((line + 1) // 2):
        turn.extend({line - 1 - k: 0, k: 0})
    for target in turn:
        for j in range(1, group):
            across(j, target).start()

    def gathered(target):
        for j in range(1, group):
            across(j, target).wait_recv()
        total = x_ref[pl.ds((row * line + target) * held, held)].astype(f32)
        for j in range(1, group):
            total = total + row_buf[j - 1, target].astype(f32)
        acc_buf[target] = total.astype(acc_buf.dtype)

    for target in turn:
        gathered(target)
        if target == line - 1:
            @pl.when(z == 0)
            def _():
                for c in range(pieces):
                    pass_buf[0, target, pl.ds(c * part, part)] = acc_buf[
                        target, pl.ds(c * part, part)
                    ]
                    along(0, target, c).start()

        if target == 0:
            @pl.when(z == line - 1)
            def _():
                for c in range(pieces):
                    pass_buf[1, target, pl.ds(c * part, part)] = acc_buf[
                        target, pl.ds(c * part, part)
                    ]
                    along(1, target, c).start()

    for k in range(line - 1):
        high, low = line - 1 - k, k
        for c in range(pieces):
            here = pl.ds(c * part, part)
            if high != line - 1:
                @pl.when((z == 0) & (high > z))
                def _():
                    pass_buf[0, high, here] = acc_buf[high, here]
                    along(0, high, c).start()

            @pl.when((z > 0) & (high > z))
            def _():
                along(0, high, c).wait_recv()
                pass_buf[0, high, here] = (
                    pass_buf[0, high, here].astype(f32) + acc_buf[high, here].astype(f32)
                ).astype(acc_buf.dtype)
                along(0, high, c).start()

            if low != 0:
                @pl.when((z == line - 1) & (low < z))
                def _():
                    pass_buf[1, low, here] = acc_buf[low, here]
                    along(1, low, c).start()

            @pl.when((z < line - 1) & (low < z))
            def _():
                along(1, low, c).wait_recv()
                pass_buf[1, low, here] = (
                    pass_buf[1, low, here].astype(f32) + acc_buf[low, here].astype(f32)
                ).astype(acc_buf.dtype)
                along(1, low, c).start()

    out_ref[...] = acc_buf[z].astype(f32)

    @pl.when(z > 0)
    def _():
        for c in range(pieces):
            here = pl.ds(c * part, part)
            along(0, z, c).wait_recv()
            out_ref[here] = out_ref[here] + pass_buf[0, z, here].astype(f32)

    @pl.when(z < line - 1)
    def _():
        for c in range(pieces):
            here = pl.ds(c * part, part)
            along(1, z, c).wait_recv()
            out_ref[here] = out_ref[here] + pass_buf[1, z, here].astype(f32)

    for target in range(line):
        for j in range(1, group):
            across(j, target).wait_send()
        for c in range(pieces):

            @pl.when(target > z)
            def _():
                along(0, target, c).wait_send()

            @pl.when(target < z)
            def _():
                along(1, target, c).wait_send()


def scatter_plane(partial):
    line, group = lax.axis_size("gz"), lax.axis_size("gy")
    held = partial.shape[0] // (line * group)
    block = partial.shape[1:]
    others = max(group - 1, 1)
    pieces = pieces_of(held)
    return pl.pallas_call(
        functools.partial(scatter_kernel, line, group),
        out_shape=jax.ShapeDtypeStruct((held,) + block, jnp.float32),
        in_specs=[VMEM],
        out_specs=VMEM,
        scratch_shapes=[
            pltpu.VMEM((others, line, held) + block, partial.dtype),
            pltpu.VMEM((line, held) + block, partial.dtype),
            pltpu.VMEM((2, line, held) + block, partial.dtype),
            pltpu.SemaphoreType.DMA((others, line)),
            pltpu.SemaphoreType.DMA((others, line)),
            pltpu.SemaphoreType.DMA((2, line, pieces)),
            pltpu.SemaphoreType.DMA((2, line, pieces)),
        ],
        compiler_params=pltpu.CompilerParams(
            collective_id=2, has_side_effects=True, vmem_limit_bytes=VMEM_LIMIT
        ),
    )(partial)


def shards(
    ham_blocks, onsite, entry_slot, send_table, reads, gram_targets, table_pick, phi, potential_in
):
    plane = lax.axis_size(PLANE)
    held, width, _ = ham_blocks.shape
    lanes_count = send_table.shape[2]
    order = onsite.shape[1]
    side = order // width
    tables = phi.shape[1]
    points = phi.shape[3]
    slots = reads.shape[1]
    pairs = pairs_of(tables)

    sent_numbers = plane * lanes_count
    own_picks = table_pick.reshape(1, -1)
    numbers = jnp.concatenate([send_table.reshape(1, -1), own_picks], axis=1)
    length = numbers.shape[1]
    room = -(-length // 1024) * 1024
    numbers = jnp.pad(numbers, ((0, 0), (0, room - length))).reshape(-1, 128)
    gathered, numbers = gather_plane(ham_blocks, numbers)
    numbers = numbers.reshape(plane, room)
    mine = lax.axis_index(PLANE)
    theirs = lax.dynamic_slice(numbers, (0, mine * lanes_count), (plane, lanes_count))
    chosen = jnp.take(theirs.reshape(-1), entry_slot[0])
    bins = ((entry_slot[0] // lanes_count) * held + chosen).astype(jnp.int32)

    density = local_call(
        functools.partial(density_kernel, side),
        jax.ShapeDtypeStruct((side, width, width), jnp.bfloat16),
        [SMEM, VMEM, VMEM],
        [
            pltpu.VMEM((order, order), jnp.float32),
            pltpu.VMEM((order, order), jnp.bfloat16),
            pltpu.VMEM((order, order), jnp.bfloat16),
        ],
        flops=4 * order**3,
        moved=gathered.size * 2,
    )(bins, gathered, onsite)
    candidates = face_stack(density)
    first_faces = faces_of(potential_in)
    source = local_call(
        source_kernel,
        jax.ShapeDtypeStruct((points // 128, 128), jnp.float32),
        [SMEM, SMEM, VMEM, VMEM],
        [
            pltpu.VMEM((tables * tables, width, width), jnp.float32),
            pltpu.VMEM((tables * width, tables * width), jnp.bfloat16),
        ],
        flops=2 * points * (tables * width) ** 2,
        moved=phi.size * 2,
    )(reads[0], table_pick[0], candidates, phi[0]).reshape(potential_in.shape)
    potential = jacobi_step(potential_in, first_faces, source)
    potential = jacobi_step(potential, faces_of(potential), source)
    grams = local_call(
        gram_kernel,
        jax.ShapeDtypeStruct((len(pairs), width, width), jnp.bfloat16),
        [VMEM, VMEM],
        [pltpu.VMEM(((tables - 1) * width, (tables - 1) * width), jnp.float32)],
        flops=2 * points * (tables * width) ** 2,
        moved=phi.size * 2,
    )(phi[0], potential.reshape(points // 128, 128))
    gathered_grams = face_stack(grams)

    before, after = both_sides(own_picks, own_picks, "gx")
    around = jnp.take(numbers[:, sent_numbers:length], neighbour_numbers(), axis=0)
    near = jnp.concatenate([own_picks, before, after, around]).reshape(7, 2, slots)
    low = jnp.minimum(near[:, 0], near[:, 1])
    high = jnp.maximum(near[:, 0], near[:, 1])
    pair = low * tables - low * (low + 1) // 2 + high - low - 1
    column = (jnp.arange(7)[:, None] * len(pairs) + pair).reshape(-1).astype(jnp.int32)
    flip = (near[:, 0] > near[:, 1]).reshape(-1).astype(jnp.int32)
    padded = jnp.concatenate([bins, jnp.full((1,), plane * held, jnp.int32)])
    place = jnp.take(padded, gram_targets[0].reshape(-1))
    partial = local_call(
        combine_kernel,
        jax.ShapeDtypeStruct((plane * held, width, width), jnp.bfloat16),
        [SMEM, SMEM, SMEM, VMEM],
        [pltpu.VMEM((plane * held, width, width), jnp.float32)],
        flops=7 * slots * width * width,
        moved=plane * held * width * width * 2,
    )(place, column, flip, gathered_grams)
    grid_blocks = scatter_plane(partial)
    return (potential, grid_blocks)


def solution(mesh):
    placed = (
        P(EVERY, None, None),
        P(EVERY, None),
        P(EVERY, None),
        P(EVERY, None, None),
        P(EVERY, None),
        P(EVERY, None, None),
        P(EVERY, None, None),
        P(EVERY, None, None, None),
        P(*EVERY),
    )
    return jax.shard_map(
        shards,
        mesh=mesh,
        in_specs=placed,
        out_specs=(P(*EVERY), P(EVERY, None, None)),
        check_vma=False,
    )
```

```python
import functools

import jax
import jax.numpy as jnp
from jax import lax
from jax.experimental import pallas as pl
from jax.experimental.pallas import tpu as pltpu
from jax.sharding import PartitionSpec as P

EPSILON = 1e-06
PLANE = ("gy", "gz")
EVERY = ("gx", "gy", "gz")
VMEM_LIMIT = 48 * 1024 * 1024
VMEM = pl.BlockSpec(memory_space=pltpu.VMEM)
SMEM = pl.BlockSpec(memory_space=pltpu.SMEM)
MESH = pl.DeviceIdType.MESH


def local_call(kernel, out_shape, in_specs, scratch=(), flops=0, moved=0, limit=24 * 1024 * 1024):
    return pl.pallas_call(
        kernel,
        out_shape=out_shape,
        in_specs=in_specs,
        out_specs=VMEM,
        scratch_shapes=scratch,
        compiler_params=pltpu.CompilerParams(vmem_limit_bytes=limit),
        cost_estimate=pl.CostEstimate(flops=flops, bytes_accessed=moved, transcendentals=0),
    )


def density_kernel(side, bins_ref, blocks_ref, onsite_ref, out_ref, h_ref, x_ref, q_ref):
    width = blocks_ref.shape[1]
    order = side * width
    rows = lax.broadcasted_iota(jnp.int32, (width, width), 0)
    columns = lax.broadcasted_iota(jnp.int32, (width, width), 1)
    unit = rows == columns
    total = jnp.zeros((width, width), jnp.float32)
    for s in range(side):
        for t in range(s, side):
            upper = blocks_ref[bins_ref[s * side + t]].astype(jnp.float32)
            lower = blocks_ref[bins_ref[t * side + s]].astype(jnp.float32)
            block = 0.5 * (upper + lower.T)
            here, there = pl.ds(s * width, width), pl.ds(t * width, width)
            if s == t:
                block = block + jnp.where(unit, onsite_ref[:, here], 0.0)
                total = total + block * block
            else:
                total = total + 2.0 * (block * block)
                h_ref[there, here] = block.T
            h_ref[here, there] = block
    norm = jnp.sum(jnp.sum(total, axis=0, keepdims=True), axis=1, keepdims=True)
    factor = lax.rsqrt(norm / order + EPSILON) / 1.3
    for s in range(side):
        here = pl.ds(s * width, width)
        x_ref[here, :] = (h_ref[here, :] * factor).astype(jnp.bfloat16)
    step = 256 if order % 256 == 0 else width
    for c in range(order // step):
        here = pl.ds(c * step, step)
        q_ref[:, here] = jnp.dot(
            x_ref[...], x_ref[:, here], preferred_element_type=jnp.float32
        ).astype(jnp.bfloat16)
    for c in range(order // step):
        here = pl.ds(c * step, step)
        h_ref[:, here] = 1.5 * x_ref[:, here].astype(jnp.float32) - 0.5 * jnp.dot(
            x_ref[...], q_ref[:, here], preferred_element_type=jnp.float32
        )
    for c in range(order // step):
        here = pl.ds(c * step, step)
        q_ref[:, here] = h_ref[:, here].astype(jnp.bfloat16)
    first = q_ref[...]
    column = q_ref[:, :width]
    inner = jnp.dot(first, column, preferred_element_type=jnp.float32).astype(jnp.bfloat16)
    outer = jnp.dot(first, inner, preferred_element_type=jnp.float32)
    result = -0.5 * (1.5 * column.astype(jnp.float32) - 0.5 * outer)
    for s in range(side):
        part = result[s * width : (s + 1) * width, :]
        if s == 0:
            part = part + jnp.where(unit, 0.5, 0.0)
        out_ref[s] = part.astype(jnp.bfloat16)


def source_kernel(reads_ref, pick_ref, blocks_ref, phi_ref, out_ref, p_ref, pb_ref):
    width = blocks_ref.shape[1]
    count = blocks_ref.shape[0]
    tables = phi_ref.shape[0]
    points = phi_ref.shape[2]
    p_ref[...] = jnp.zeros_like(p_ref)
    for r in range(reads_ref.shape[0]):
        code = reads_ref[r]

        @pl.when(code < count)
        def _():
            place = pick_ref[0, r] * tables + pick_ref[1, r]
            p_ref[place] = p_ref[place] + blocks_ref[code].astype(jnp.float32)

    for a in range(tables):
        for b in range(tables):
            pb_ref[a * width : (a + 1) * width, b * width : (b + 1) * width] = p_ref[
                a * tables + b
            ].astype(jnp.bfloat16)
    step = 512

    def body(c, carry):
        here = pl.ds(pl.multiple_of(c * step, step), step)
        cells = phi_ref[:, :, here].reshape(tables * width, step)
        mixed = jnp.dot(pb_ref[...], cells, preferred_element_type=jnp.float32)
        line = jnp.sum(mixed * cells.astype(jnp.float32), axis=0, keepdims=True)
        for j in range(step // 128):
            out_ref[pl.ds(c * (step // 128) + j, 1), :] = line[:, j * 128 : (j + 1) * 128]
        return carry

    lax.fori_loop(0, points // step, body, 0)


def pairs_of(tables):
    return [(a, b) for a in range(tables) for b in range(a + 1, tables)]


def gram_kernel(phi_ref, v_ref, out_ref, g_ref):
    tables, width, points = phi_ref.shape
    step = 512
    g_ref[...] = jnp.zeros_like(g_ref)
    size = (tables - 1) * width

    def body(c, carry):
        here = pl.ds(pl.multiple_of(c * step, step), step)
        rows = v_ref[pl.ds(c * (step // 128), step // 128), :]
        line = jnp.concatenate([rows[j : j + 1, :] for j in range(step // 128)], axis=1)
        right = phi_ref[1:, :, here].reshape(size, step).astype(jnp.float32)
        weighted = (right * line).astype(jnp.bfloat16)
        left = phi_ref[: tables - 1, :, here].reshape(size, step)
        g_ref[...] += lax.dot_general(
            left, weighted, (((1,), (1,)), ((), ())), preferred_element_type=jnp.float32
        )
        return carry

    lax.fori_loop(0, points // step, body, 0)
    for n, (a, b) in enumerate(pairs_of(tables)):
        out_ref[n] = g_ref[
            a * width : (a + 1) * width, (b - 1) * width : b * width
        ].astype(jnp.bfloat16)


def combine_kernel(bin_ref, col_ref, flip_ref, blocks_ref, out_ref, acc_ref):
    bins = out_ref.shape[0]
    acc_ref[...] = jnp.zeros_like(acc_ref)

    def body(n, carry):
        place = bin_ref[n]

        @pl.when((place < bins) & (flip_ref[n] == 0))
        def _():
            acc_ref[place] = acc_ref[place] + blocks_ref[col_ref[n]].astype(jnp.float32)

        @pl.when((place < bins) & (flip_ref[n] == 1))
        def _():
            acc_ref[place] = acc_ref[place] + blocks_ref[col_ref[n]].astype(jnp.float32).T

        return carry

    lax.fori_loop(0, bin_ref.shape[0], body, 0)
    out_ref[...] = acc_ref[...].astype(jnp.bfloat16)


def face_kernel(counts, kinds, *refs):
    ins, outs = refs[:kinds], refs[kinds : 2 * kinds]
    send_sem, recv_sem = refs[2 * kinds :]
    barrier = pltpu.get_barrier_semaphore()
    copies = []
    for n, (axis, count) in enumerate(zip(EVERY, counts)):
        here = lax.axis_index(axis)
        for face, step in ((2 * n + 1, 1), (2 * n + 2, count - 1)):
            if count == 1 or (count == 2 and face % 2 == 0):
                continue
            copies.append((axis, lax.rem(here + step, count), face))
    for axis, peer, _ in copies:
        pl.semaphore_signal(barrier, inc=1, device_id={axis: peer}, device_id_type=MESH)
    pl.semaphore_wait(barrier, len(copies))
    started = []
    for i in range(kinds):
        for axis, peer, face in sorted(copies, key=lambda item: item[0] == "gy"):
            copy = pltpu.make_async_remote_copy(
                src_ref=ins[i],
                dst_ref=outs[i].at[face],
                send_sem=send_sem.at[i, face],
                recv_sem=recv_sem.at[i, face],
                device_id={axis: peer},
                device_id_type=MESH,
            )
            copy.start()
            started.append(copy)
    for i in range(kinds):
        outs[i][0] = ins[i][...]
        for n, count in enumerate(counts):
            if count == 1:
                outs[i][2 * n + 1] = ins[i][...]
                outs[i][2 * n + 2] = ins[i][...]
    for copy in started:
        copy.wait_recv()
    for i in range(kinds):
        for n, count in enumerate(counts):
            if count == 2:
                outs[i][2 * n + 2] = outs[i][2 * n + 1]
    for copy in started:
        copy.wait_send()


def face_stack(number, *arrays):
    counts = [lax.axis_size(axis) for axis in EVERY]
    kinds = len(arrays)
    return pl.pallas_call(
        functools.partial(face_kernel, counts, kinds),
        out_shape=tuple(jax.ShapeDtypeStruct((7,) + a.shape, a.dtype) for a in arrays),
        in_specs=[VMEM] * kinds,
        out_specs=(VMEM,) * kinds,
        scratch_shapes=[
            pltpu.SemaphoreType.DMA((kinds, 7)),
            pltpu.SemaphoreType.DMA((kinds, 7)),
        ],
        compiler_params=pltpu.CompilerParams(
            collective_id=number, has_side_effects=True, vmem_limit_bytes=12 * 1024 * 1024
        ),
    )(*arrays)


def jacobi_step(fields, source):
    field = fields[0]
    beside_all = source
    for dim in range(3):
        size = field.shape[dim]
        below = lax.slice_in_dim(fields[2 * dim + 1], size - 1, size, axis=dim)
        above = lax.slice_in_dim(fields[2 * dim + 2], 0, 1, axis=dim)
        beside_all = beside_all + jnp.concatenate(
            [below, lax.slice_in_dim(field, 0, size - 1, axis=dim)], axis=dim
        )
        beside_all = beside_all + jnp.concatenate(
            [lax.slice_in_dim(field, 1, size, axis=dim), above], axis=dim
        )
    return beside_all / 6.0


def greet_plane(line, group, z, row):
    barrier = pltpu.get_barrier_semaphore()

    @pl.when(z > 0)
    def _():
        pl.semaphore_signal(barrier, inc=1, device_id={"gz": z - 1}, device_id_type=MESH)

    @pl.when(z < line - 1)
    def _():
        pl.semaphore_signal(barrier, inc=1, device_id={"gz": z + 1}, device_id_type=MESH)

    for j in range(1, group):
        pl.semaphore_signal(
            barrier, inc=1, device_id={"gy": lax.rem(row + j, group)}, device_id_type=MESH
        )

    below = lax.div(z + line - 1, line)
    above = lax.div(2 * line - 2 - z, line)
    pl.semaphore_wait(barrier, group - 1 + below + above)


def pieces_of(count):
    return 4 if count % 4 == 0 else 1


def gather_kernel(
    line, group, x_ref, n_ref, out_ref, nout_ref, line_send, line_recv, row_send, row_recv
):
    z, row = lax.axis_index("gz"), lax.axis_index("gy")
    held, tall = x_ref.shape[0], n_ref.shape[0]
    pieces = pieces_of(held)
    part = held // pieces

    def slot(owner_row, owner_z, c):
        owner = owner_row * line + owner_z
        if c < pieces:
            return out_ref.at[pl.ds(owner * held + c * part, part)]
        return nout_ref.at[pl.ds(pl.multiple_of(owner * tall, tall), tall)]

    def source(c):
        return x_ref.at[pl.ds(c * part, part)] if c < pieces else n_ref

    def along(origin, c, side, own):
        return pltpu.make_async_remote_copy(
            src_ref=source(c) if own else slot(row, origin, c),
            dst_ref=slot(row, origin, c),
            send_sem=line_send.at[side, origin, c],
            recv_sem=line_recv.at[origin, c],
            device_id={"gz": z + 1 if side == 0 else z - 1},
            device_id_type=MESH,
        )

    def across(j, origin, kind, own):
        owner = row * line + origin
        if kind == 0:
            dst = out_ref.at[pl.ds(owner * held, held)]
            src = x_ref if own else dst
        else:
            dst = nout_ref.at[pl.ds(pl.multiple_of(owner * tall, tall), tall)]
            src = n_ref if own else dst
        return pltpu.make_async_remote_copy(
            src_ref=src,
            dst_ref=dst,
            send_sem=row_send.at[j - 1, origin, kind],
            recv_sem=row_recv.at[j - 1, origin, kind],
            device_id={"gy": lax.rem(row + j, group)},
            device_id_type=MESH,
        )

    def arrived(j, origin, kind):
        owner = lax.rem(row + group - j, group) * line + origin
        if kind == 0:
            dst = out_ref.at[pl.ds(owner * held, held)]
        else:
            dst = nout_ref.at[pl.ds(pl.multiple_of(owner * tall, tall), tall)]
        return pltpu.make_async_remote_copy(
            src_ref=dst,
            dst_ref=dst,
            send_sem=row_send.at[j - 1, origin, kind],
            recv_sem=row_recv.at[j - 1, origin, kind],
            device_id={"gy": lax.rem(row + j, group)},
            device_id_type=MESH,
        )

    greet_plane(line, group, z, row)
    order = [pieces] + list(range(pieces))
    for c in order:

        @pl.when(z < line - 1)
        def _():
            along(z, c, 0, True).start()

        @pl.when(z > 0)
        def _():
            along(z, c, 1, True).start()

    for j in range(1, group):
        for kind in range(2):
            across(j, z, kind, True).start()
    mine = row * line + z
    out_ref[pl.ds(mine * held, held)] = x_ref[...]
    nout_ref[pl.ds(pl.multiple_of(mine * tall, tall), tall), :] = n_ref[...]
    for s in range(1, line):
        for c in order:

            @pl.when(z >= s)
            def _():
                along(z - s, c, 0, False).wait_recv()

            @pl.when((z >= s) & (z < line - 1))
            def _():
                along(z - s, c, 0, False).start()

            @pl.when(z + s < line)
            def _():
                along(z + s, c, 1, False).wait_recv()

            @pl.when((z + s < line) & (z > 0))
            def _():
                along(z + s, c, 1, False).start()

        for j in range(1, group):
            for kind in range(2):

                @pl.when(z >= s)
                def _():
                    across(j, z - s, kind, False).start()

                @pl.when(z + s < line)
                def _():
                    across(j, z + s, kind, False).start()

    for j in range(1, group):
        for origin in range(line):
            for kind in range(2):
                arrived(j, origin, kind).wait_recv()
                across(j, origin, kind, False).wait_send()
    for s in range(line):
        for c in order:

            @pl.when((z >= s) & (z < line - 1))
            def _():
                along(z - s, c, 0, False).wait_send()

            @pl.when((z + s < line) & (z > 0))
            def _():
                along(z + s, c, 1, False).wait_send()


def gather_plane(blocks, numbers):
    line, group = lax.axis_size("gz"), lax.axis_size("gy")
    plane = line * group
    kinds = pieces_of(blocks.shape[0]) + 1
    others = max(group - 1, 1)
    return pl.pallas_call(
        functools.partial(gather_kernel, line, group),
        out_shape=(
            jax.ShapeDtypeStruct((plane * blocks.shape[0],) + blocks.shape[1:], blocks.dtype),
            jax.ShapeDtypeStruct((plane * numbers.shape[0], numbers.shape[1]), numbers.dtype),
        ),
        in_specs=[VMEM, VMEM],
        out_specs=(VMEM, VMEM),
        scratch_shapes=[
            pltpu.SemaphoreType.DMA((2, line, kinds)),
            pltpu.SemaphoreType.DMA((line, kinds)),
            pltpu.SemaphoreType.DMA((others, line, 2)),
            pltpu.SemaphoreType.DMA((others, line, 2)),
        ],
        compiler_params=pltpu.CompilerParams(
            collective_id=1, has_side_effects=True, vmem_limit_bytes=min(3 * blocks.nbytes * plane + 2**23, VMEM_LIMIT)
        ),
    )(blocks, numbers)


def scatter_kernel(
    line, group, x_ref, out_ref, row_buf, acc_buf, pass_buf,
    row_send, row_recv, line_send, line_recv,
):
    z, row = lax.axis_index("gz"), lax.axis_index("gy")
    held = out_ref.shape[0]
    pieces = pieces_of(held)
    part = held // pieces
    f32 = jnp.float32

    def across(j, target):
        peer = lax.rem(row + j, group)
        return pltpu.make_async_remote_copy(
            src_ref=x_ref.at[pl.ds((peer * line + target) * held, held)],
            dst_ref=row_buf.at[j - 1, target],
            send_sem=row_send.at[j - 1, target],
            recv_sem=row_recv.at[j - 1, target],
            device_id={"gy": peer},
            device_id_type=MESH,
        )

    def along(side, target, c):
        piece = pass_buf.at[side, target, pl.ds(c * part, part)]
        return pltpu.make_async_remote_copy(
            src_ref=piece,
            dst_ref=piece,
            send_sem=line_send.at[side, target, c],
            recv_sem=line_recv.at[side, target, c],
            device_id={"gz": z + 1 if side == 0 else z - 1},
            device_id_type=MESH,
        )

    greet_plane(line, group, z, row)
    turn = []
    for k in range((line + 1) // 2):
        turn.extend({line - 1 - k: 0, k: 0})
    for target in turn:
        for j in range(1, group):
            across(j, target).start()

    def gathered(target):
        for j in range(1, group):
            across(j, target).wait_recv()
        total = x_ref[pl.ds((row * line + target) * held, held)].astype(f32)
        for j in range(1, group):
            total = total + row_buf[j - 1, target].astype(f32)
        acc_buf[target] = total.astype(acc_buf.dtype)

    for target in turn:
        gathered(target)
        if target == line - 1:
            @pl.when(z == 0)
            def _():
                for c in range(pieces):
                    pass_buf[0, target, pl.ds(c * part, part)] = acc_buf[
                        target, pl.ds(c * part, part)
                    ]
                    along(0, target, c).start()

        if target == 0:
            @pl.when(z == line - 1)
            def _():
                for c in range(pieces):
                    pass_buf[1, target, pl.ds(c * part, part)] = acc_buf[
                        target, pl.ds(c * part, part)
                    ]
                    along(1, target, c).start()

    for k in range(line - 1):
        high, low = line - 1 - k, k
        for c in range(pieces):
            here = pl.ds(c * part, part)
            if high != line - 1:
                @pl.when((z == 0) & (high > z))
                def _():
                    pass_buf[0, high, here] = acc_buf[high, here]
                    along(0, high, c).start()

            @pl.when((z > 0) & (high > z))
            def _():
                along(0, high, c).wait_recv()
                pass_buf[0, high, here] = (
                    pass_buf[0, high, here].astype(f32) + acc_buf[high, here].astype(f32)
                ).astype(acc_buf.dtype)
                along(0, high, c).start()

            if low != 0:
                @pl.when((z == line - 1) & (low < z))
                def _():
                    pass_buf[1, low, here] = acc_buf[low, here]
                    along(1, low, c).start()

            @pl.when((z < line - 1) & (low < z))
            def _():
                along(1, low, c).wait_recv()
                pass_buf[1, low, here] = (
                    pass_buf[1, low, here].astype(f32) + acc_buf[low, here].astype(f32)
                ).astype(acc_buf.dtype)
                along(1, low, c).start()

    out_ref[...] = acc_buf[z].astype(f32)

    @pl.when(z > 0)
    def _():
        for c in range(pieces):
            here = pl.ds(c * part, part)
            along(0, z, c).wait_recv()
            out_ref[here] = out_ref[here] + pass_buf[0, z, here].astype(f32)

    @pl.when(z < line - 1)
    def _():
        for c in range(pieces):
            here = pl.ds(c * part, part)
            along(1, z, c).wait_recv()
            out_ref[here] = out_ref[here] + pass_buf[1, z, here].astype(f32)

    for target in range(line):
        for j in range(1, group):
            across(j, target).wait_send()
        for c in range(pieces):

            @pl.when(target > z)
            def _():
                along(0, target, c).wait_send()

            @pl.when(target < z)
            def _():
                along(1, target, c).wait_send()


def scatter_plane(partial):
    line, group = lax.axis_size("gz"), lax.axis_size("gy")
    held = partial.shape[0] // (line * group)
    block = partial.shape[1:]
    others = max(group - 1, 1)
    pieces = pieces_of(held)
    return pl.pallas_call(
        functools.partial(scatter_kernel, line, group),
        out_shape=jax.ShapeDtypeStruct((held,) + block, jnp.float32),
        in_specs=[VMEM],
        out_specs=VMEM,
        scratch_shapes=[
            pltpu.VMEM((others, line, held) + block, partial.dtype),
            pltpu.VMEM((line, held) + block, partial.dtype),
            pltpu.VMEM((2, line, held) + block, partial.dtype),
            pltpu.SemaphoreType.DMA((others, line)),
            pltpu.SemaphoreType.DMA((others, line)),
            pltpu.SemaphoreType.DMA((2, line, pieces)),
            pltpu.SemaphoreType.DMA((2, line, pieces)),
        ],
        compiler_params=pltpu.CompilerParams(
            collective_id=2, has_side_effects=True, vmem_limit_bytes=VMEM_LIMIT
        ),
    )(partial)


def shards(
    ham_blocks, onsite, entry_slot, send_table, reads, gram_targets, table_pick, phi, potential_in
):
    plane = lax.axis_size(PLANE)
    held, width, _ = ham_blocks.shape
    lanes_count = send_table.shape[2]
    order = onsite.shape[1]
    side = order // width
    tables = phi.shape[1]
    points = phi.shape[3]
    slots = reads.shape[1]
    pairs = pairs_of(tables)

    sent_numbers = plane * lanes_count
    own_picks = table_pick.reshape(1, -1)
    numbers = jnp.concatenate([send_table.reshape(1, -1), own_picks], axis=1)
    length = numbers.shape[1]
    room = -(-length // 1024) * 1024
    numbers = jnp.pad(numbers, ((0, 0), (0, room - length))).reshape(-1, 128)
    own_numbers = numbers
    gathered, numbers = gather_plane(ham_blocks, numbers)
    numbers = numbers.reshape(plane, room)
    mine = lax.axis_index(PLANE)
    theirs = lax.dynamic_slice(numbers, (0, mine * lanes_count), (plane, lanes_count))
    chosen = jnp.take(theirs.reshape(-1), entry_slot[0])
    bins = ((entry_slot[0] // lanes_count) * held + chosen).astype(jnp.int32)

    density = local_call(
        functools.partial(density_kernel, side),
        jax.ShapeDtypeStruct((side, width, width), jnp.bfloat16),
        [SMEM, VMEM, VMEM],
        [
            pltpu.VMEM((order, order), jnp.float32),
            pltpu.VMEM((order, order), jnp.bfloat16),
            pltpu.VMEM((order, order), jnp.bfloat16),
        ],
        flops=4 * order**3,
        moved=gathered.size * 2,
    )(bins, gathered, onsite)
    candidates, fields, around = face_stack(3, density, potential_in, own_numbers)
    candidates = candidates.reshape(7 * side, width, width)
    source = local_call(
        source_kernel,
        jax.ShapeDtypeStruct((points // 128, 128), jnp.float32),
        [SMEM, SMEM, VMEM, VMEM],
        [
            pltpu.VMEM((tables * tables, width, width), jnp.float32),
            pltpu.VMEM((tables * width, tables * width), jnp.bfloat16),
        ],
        flops=2 * points * (tables * width) ** 2,
        moved=phi.size * 2,
    )(reads[0], table_pick[0], candidates, phi[0]).reshape(potential_in.shape)
    potential = jacobi_step(fields, source)
    potential = jacobi_step(face_stack(4, potential)[0], source)
    grams = local_call(
        gram_kernel,
        jax.ShapeDtypeStruct((len(pairs), width, width), jnp.bfloat16),
        [VMEM, VMEM],
        [pltpu.VMEM(((tables - 1) * width, (tables - 1) * width), jnp.float32)],
        flops=2 * points * (tables * width) ** 2,
        moved=phi.size * 2,
    )(phi[0], potential.reshape(points // 128, 128))
    gathered_grams = face_stack(5, grams)[0].reshape(7 * len(pairs), width, width)

    near = around.reshape(7, room)[:, sent_numbers:length].reshape(7, 2, slots)
    low = jnp.minimum(near[:, 0], near[:, 1])
    high = jnp.maximum(near[:, 0], near[:, 1])
    pair = low * tables - low * (low + 1) // 2 + high - low - 1
    column = (jnp.arange(7)[:, None] * len(pairs) + pair).reshape(-1).astype(jnp.int32)
    flip = (near[:, 0] > near[:, 1]).reshape(-1).astype(jnp.int32)
    padded = jnp.concatenate([bins, jnp.full((1,), plane * held, jnp.int32)])
    place = jnp.take(padded, gram_targets[0].reshape(-1))
    partial = local_call(
        combine_kernel,
        jax.ShapeDtypeStruct((plane * held, width, width), jnp.bfloat16),
        [SMEM, SMEM, SMEM, VMEM],
        [pltpu.VMEM((plane * held, width, width), jnp.float32)],
        flops=7 * slots * width * width,
        moved=plane * held * width * width * 2,
        limit=min(7 * plane * held * width * width + 2**23, VMEM_LIMIT),
    )(place, column, flip, gathered_grams)
    grid_blocks = scatter_plane(partial)
    return (potential, grid_blocks)


def solution(mesh):
    placed = (
        P(EVERY, None, None),
        P(EVERY, None),
        P(EVERY, None),
        P(EVERY, None, None),
        P(EVERY, None),
        P(EVERY, None, None),
        P(EVERY, None, None),
        P(EVERY, None, None, None),
        P(*EVERY),
    )
    return jax.shard_map(
        shards,
        mesh=mesh,
        in_specs=placed,
        out_specs=(P(*EVERY), P(EVERY, None, None)),
        check_vma=False,
    )
```
